256 devices in a mesh: seq: 16 (over x_lo, y, core), exp: 16 (over x_hi, z).
Axes of the slice: x: 4 (x_hi: 2, x_lo: 2; x = x_hi * 2 + x_lo), y: 4, z: 8, core: 2. Of those that a mesh axis runs over, the one named last changes fastest.
Arguments:
- q_nope: bfloat16 [1024, 16384], P('seq', 'exp'), may hold values from -6 to 6
- q_rope: bfloat16 [1024, 8192], P('seq', 'exp'), may hold values from -8 to 8
- slab_latent: bfloat16 [1024, 512], P('seq'), may hold values from -6 to 6
- slab_rope: bfloat16 [1024, 64], P('seq'), may hold values from -6 to 6
- kv_gain: float32 [512], replicated, may hold values from 0.1 to 1.9
- cache_latent: bfloat16 [1024, 512], P('seq'), may hold values from -6 to 6
- cache_rope: bfloat16 [1024, 64], P('seq'), may hold values from -8 to 8
- w_uk: bfloat16 [128, 128, 512], P('exp'), may hold values from -0.5 to 0.5
- w_uv: bfloat16 [128, 512, 128], P('exp'), may hold values from -1.5 to 1.5
- prev_rows: bfloat16 [768, 5120], P('exp'), may hold values from -6 to 6
- expert_ids: int32 [768, 6], P('exp'), may hold values from 0 to 15, all different within a row; in each aligned block of 48 rows (0 to 47, 48 to 95, ...) at most 24 rows name the same one
- gate_scores: float32 [768, 6], P('exp'), may hold values from 0.02 to 0.5
- w_gate: bfloat16 [16, 1536, 5120], P('exp', 'seq'), may hold values from -0.078125 to 0.078125
- w_up: bfloat16 [16, 1536, 5120], P('exp', 'seq'), may hold values from -0.078125 to 0.078125
- w_down: bfloat16 [16, 1536, 5120], P('exp', 'seq'), may hold values from -0.21875 to 0.21875
Outputs:
- attn_out: bfloat16 [1024, 16384], P('seq', 'exp')
- moe_out: bfloat16 [768, 5120], P('exp', 'seq')
The draws below stay inside these ranges and needn't reach their ends.
Inputs may be any that keep to these rules, and one draw needn't show every extreme that they name: `expert_ids`: each row names 6 different experts; in each aligned block of 48 rows no expert is named by more than 24 rows, and in some block one expert is named by exactly 24.
All inputs are finite; a program needn't handle non-finite values.
Results may differ from the reference program's by a relative error of at most 0.015.
Values may be sent and summed in bfloat16 or wider, within the bound.
No kernel may reach another device: no remote copies, remote signals or barrier semaphores. Data moves between devices by JAX's collectives and lax.ppermute only.
A program may use at most 128 MiB of HBM per device.

```python
import math
import jax
import jax.numpy as jnp
import numpy as np
from jax import lax

D = 5120
FF = 1536
H = 128
NOPE = 128
ROPE = 64
VD = 128
KVL = 512
TOP = 6
ROW_DEV = 48
EXPERTS = 16
TOKENS = 1024
CTX = 1024
ROWS = 768
CAP = 24
N_EXP = 16


def draw_q_rope(key, part):
    key = jax.random.fold_in(key, 11)
    values = jnp.clip(jax.random.normal(key, (TOKENS, H, ROPE), jnp.float32), -8.0, 8.0)
    return values.reshape(TOKENS, H * ROPE).astype(jnp.bfloat16)


def draw_cache_rope(key, part):
    key = jax.random.fold_in(key, 23)
    values = jnp.clip(jax.random.normal(key, (CTX, ROPE), jnp.float32), -8.0, 8.0)
    return values.astype(jnp.bfloat16)


def with_spikes(array, own_key, source, target, shards_of, factor):
    def block_of(dim):
        return (jnp.arange(array.shape[dim]) // (array.shape[dim] // shards_of)).reshape((-1,) + (1,) * (array.ndim - 1 - dim))

    near = jax.random.permutation(own_key, shards_of)[block_of(target)]
    second = (block_of(target) + shards_of // 2) % shards_of
    return jnp.where((block_of(source) == near) | (block_of(source) == second), factor * array, array)


def level_of(stream_key, shape, cuts, smallest, high):
    loudness = 1.0
    for dim, parts in cuts:
        steps = jax.random.uniform(jax.random.fold_in(jax.random.fold_in(stream_key, 6), dim), (parts,), jnp.float32, smallest / len(cuts), high / len(cuts))
        loudness = loudness * jnp.repeat(jnp.exp(steps), shape[dim] // parts).reshape((-1,) + (1,) * (len(shape) - 1 - dim))
    return loudness


def deal_out(key, own, number, rows, number_of, top, most, skew):
    sequence = jax.random.permutation(key, number_of)
    crowded, ordinary = load_shares(number_of, rows * top, most, skew, True), load_shares(number_of, rows * top, most, skew, False)
    places = jnp.arange(number_of)

    def named(sizes, turn):
        used = int((sizes > 0).sum())
        fixed = max(1, used // 4)
        passed = fixed + (places - fixed + turn * (used - fixed)) % max(1, number_of - fixed)
        return jnp.zeros((number_of,), jnp.int32).at[sequence[jnp.where(places < fixed, places, passed)]].set(jnp.asarray(sizes, jnp.int32))

    sizes = jnp.where(number % 4 == 0, named(crowded, number // 4), named(ordinary, number - number // 4 - 1))
    mixed = jax.random.permutation(jax.random.fold_in(own, 3), number_of)
    donor, receiver = mixed[0:number_of // 2 * 2:2], mixed[1:number_of // 2 * 2:2]
    slack = jnp.minimum(sizes[donor] - 1, most - sizes[receiver]) // 2
    slack = jnp.where((donor == sequence[0]) | (receiver == sequence[0]) | (sizes[receiver] == 0), 0, jnp.maximum(slack, 0))
    passed = jax.random.randint(jax.random.fold_in(own, 4), (number_of // 2,), 0, 1 << 20) % (slack + 1)
    sizes = sizes.at[donor].add(-passed).at[receiver].add(passed)
    labels = jnp.searchsorted(jnp.cumsum(sizes), jnp.arange(rows * top), side="right").astype(jnp.int32)
    listing = labels.reshape(top, rows).T
    listing = listing[jax.random.permutation(jax.random.fold_in(own, 1), rows)]
    turn = jax.random.randint(jax.random.fold_in(own, 2), (rows, 1), 0, top)
    return jnp.take_along_axis(listing, (jnp.arange(top)[None, :] + turn) % top, axis=1)


def load_shares(amount, total, most, slope, full):
    loads = [(1 << 20) // math.isqrt(grade ** slope) + 1 for grade in range(1, amount + 1)]
    largest = most if full else min(most, max(-(-total // amount), total * loads[0] // sum(loads)))
    least = 1 if total - largest >= amount - 1 else 0
    given, surplus = [largest] + [least] * (amount - 1), total - largest - least * (amount - 1)
    while surplus > 0:
        free = [i for i in range(1, amount) if given[i] < largest] or [i for i in range(1, amount) if given[i] < most]
        whole, remaining = sum([loads[i] for i in free]), surplus
        for i in free:
            addition = min(most - given[i], max(1, remaining * loads[i] // whole), surplus)
            given[i] = given[i] + addition
            surplus = surplus - addition
    return np.array(given)


def gaussian(rng, dims, scale, limit, cuts=(), held_as=jnp.bfloat16):
    result = jax.random.normal(rng, dims, jnp.float32) * scale
    if len(cuts) > 0:
        result = level_of(rng, dims, cuts, -0.22, 0.18) * result
    return jnp.clip(result, min=-limit, max=limit).astype(held_as)


def gaussian_with(stream_key, dims, width, reach, split, heavy, held_as=jnp.bfloat16):
    drawn = width * jax.random.normal(stream_key, dims, jnp.float32)
    if split:
        drawn = drawn * level_of(stream_key, dims, split, -0.22, 0.18)
    return jnp.clip(with_spikes(drawn, jax.random.fold_in(stream_key, 3), *heavy), -reach, reach).astype(held_as)


def setup_inputs(seed: int = 0) -> dict:
    key_list = jax.random.split(jax.random.key(seed), 16)
    q_nope = gaussian(key_list[0], (TOKENS, H * NOPE), 1.0, 6.0, ((0, 16), (1, 16)))
    q_rope = draw_q_rope(jax.random.fold_in(key_list[15], 71), 0)
    slab_latent = gaussian(key_list[2], (TOKENS, KVL), 1.0, 6.0, ((0, 16),))
    slab_rope = gaussian(key_list[3], (TOKENS, ROPE), 1.0, 6.0, ((0, 16),))
    kv_gain = jnp.clip(1.0 + 0.18 * jax.random.normal(key_list[4], (KVL,), jnp.float32), 0.1, 1.9)
    cache_latent = gaussian(key_list[5], (CTX, KVL), 1.0, 6.0, ((0, 16),))
    cache_rope = draw_cache_rope(jax.random.fold_in(key_list[15], 71), 0)
    w_uk = gaussian(key_list[7], (H, NOPE, KVL), NOPE ** -0.5, 0.5, ((0, 16),))
    w_uv = gaussian(key_list[8], (H, KVL, VD), 16 ** -0.5, 1.5, ((0, 16),))
    prev_rows = gaussian(key_list[9], (ROWS, D), 1.0, 6.0, ((0, 16),))
    expert_ids_keys = jax.random.split(jax.random.fold_in(key_list[10], 1), ROWS // ROW_DEV)
    expert_ids_turns = jax.random.permutation(jax.random.fold_in(key_list[10], 3), ROWS // ROW_DEV)
    expert_ids = jax.vmap(lambda own, number: deal_out(jax.random.fold_in(key_list[10], 2), own, number, ROW_DEV, EXPERTS, TOP, CAP, 1))(expert_ids_keys, expert_ids_turns).reshape((ROWS, TOP))
    gate_scores = jnp.clip(jnp.exp(math.log(0.5) - 3.218876 * jax.random.uniform(key_list[11], (ROWS, TOP), jnp.float32) ** level_of(key_list[11], (ROWS, TOP), ((0, 16),), -0.2, 0.2)), 0.02, 0.5)
    w_gate = gaussian(key_list[12], (EXPERTS, FF, D), D ** -0.5, 0.078125, ((0, 16), (1, 16)))
    w_up = gaussian(key_list[13], (EXPERTS, FF, D), D ** -0.5, 0.078125, ((0, 16), (1, 16)))
    w_down = gaussian_with(key_list[14], (EXPERTS, FF, D), FF ** -0.5, 0.21875, ((0, 16), (1, 16)), (1, 2, 16, 2.0))
    return {"q_nope": q_nope, "q_rope": q_rope, "slab_latent": slab_latent, "slab_rope": slab_rope, "kv_gain": kv_gain, "cache_latent": cache_latent, "cache_rope": cache_rope, "w_uk": w_uk, "w_uv": w_uv, "prev_rows": prev_rows, "expert_ids": expert_ids, "gate_scores": gate_scores, "w_gate": w_gate, "w_up": w_up, "w_down": w_down}


eps = 1e-06

def latent_norm(latent, kv_gain):
    values = latent.astype(jnp.float32)
    spread = lax.rsqrt(lax.optimization_barrier(jnp.mean(values * values, axis=-1, keepdims=True)) + eps)
    return (values * spread * kv_gain).astype(jnp.bfloat16)

def expert_slots(expert_ids, experts, capacity):
    row_count, top_count = expert_ids.shape
    flat_ids = expert_ids.reshape(row_count * top_count)
    onehot = (flat_ids[:, None] == jnp.arange(experts, dtype=jnp.int32)[None, :]).astype(jnp.int32)
    rank_in_expert = lax.optimization_barrier(jnp.sum((jnp.cumsum(onehot, axis=0) - 1) * onehot, axis=1))
    return flat_ids * capacity + rank_in_expert

def reference(q_nope, q_rope, slab_latent, slab_rope, kv_gain, cache_latent, cache_rope, w_uk, w_uv, prev_rows, expert_ids, gate_scores, w_gate, w_up, w_down):
    score_scale = (NOPE + ROPE) ** (-0.5)
    slab_keys = latent_norm(slab_latent, kv_gain)
    keys_latent = jnp.concatenate([cache_latent, slab_keys], axis=0)
    keys_rope = jnp.concatenate([cache_rope, slab_rope], axis=0)
    query_pos = CTX + jnp.arange(TOKENS, dtype=jnp.int32)
    key_pos = jnp.arange(CTX + TOKENS, dtype=jnp.int32)
    visible = key_pos[None, :] <= query_pos[:, None]
    nope_heads = jnp.transpose(q_nope.reshape(TOKENS, H, NOPE), (1, 0, 2))
    rope_heads = jnp.transpose(q_rope.reshape(TOKENS, H, ROPE), (1, 0, 2))

    def one_head(operands):
        nope_part, rope_part, absorb, value_up = operands
        query_latent = jnp.dot(nope_part, absorb, preferred_element_type=jnp.float32).astype(jnp.bfloat16)
        scores = jnp.dot(query_latent, keys_latent.T, preferred_element_type=jnp.float32)
        scores = scores + jnp.dot(rope_part, keys_rope.T, preferred_element_type=jnp.float32)
        scores = jnp.where(visible, scores * score_scale, -jnp.inf)
        row_peak = lax.optimization_barrier(jnp.max(scores, axis=1, keepdims=True))
        weights = jnp.exp(scores - row_peak)
        row_total = lax.optimization_barrier(jnp.sum(weights, axis=1, keepdims=True))
        mixed_latent = jnp.dot(weights.astype(jnp.bfloat16), keys_latent, preferred_element_type=jnp.float32) / row_total
        return jnp.dot(mixed_latent.astype(jnp.bfloat16), value_up, preferred_element_type=jnp.float32).astype(jnp.bfloat16)
    head_out = lax.map(one_head, (nope_heads, rope_heads, w_uk, w_uv))
    attn_out = jnp.transpose(head_out, (1, 0, 2)).reshape(TOKENS, H * VD)
    capacity = CAP
    block_ids = expert_ids.reshape(N_EXP, ROW_DEV, TOP)
    slot_index = jax.vmap(lambda ids_block: expert_slots(ids_block, EXPERTS, capacity))(block_ids)
    source_row = jnp.arange(N_EXP, dtype=jnp.int32)[:, None] * ROW_DEV + jnp.arange(ROW_DEV * TOP, dtype=jnp.int32)[None, :] // TOP
    block_index = jnp.broadcast_to(jnp.arange(N_EXP, dtype=jnp.int32)[:, None], slot_index.shape)
    row_table = jnp.zeros((N_EXP, EXPERTS * capacity), jnp.int32).at[block_index, slot_index].set(source_row)
    row_table = jnp.transpose(row_table.reshape(N_EXP, EXPERTS, capacity), (1, 0, 2)).reshape(EXPERTS, N_EXP * capacity)

    def expert_pass(operands):
        rows_index, gate_weight, up_weight, down_weight = operands
        chosen = prev_rows[rows_index]
        gate_act = jnp.dot(chosen, gate_weight.T, preferred_element_type=jnp.float32)
        up_act = jnp.dot(chosen, up_weight.T, preferred_element_type=jnp.float32)
        hidden = (jax.nn.silu(gate_act) * up_act).astype(jnp.bfloat16)
        return jnp.dot(hidden, down_weight, preferred_element_type=jnp.float32)
    results = lax.map(expert_pass, (row_table, w_gate, w_up, w_down))
    results = results.reshape(EXPERTS, N_EXP, capacity, D)
    flat_ids = expert_ids.reshape(N_EXP, ROW_DEV * TOP)
    slot_rank = slot_index - flat_ids * capacity
    picked = results[flat_ids, block_index, slot_rank].reshape(ROWS, TOP, D)
    moe_out = lax.optimization_barrier(jnp.sum(gate_scores[:, :, None] * picked, axis=1)).astype(jnp.bfloat16)
    return (attn_out, moe_out)
```

```python
import functools
import jax
import jax.numpy as jnp
from jax import lax
from jax.experimental import pallas as pl
from jax.experimental.pallas import tpu as pltpu
from jax.sharding import Mesh, PartitionSpec as P

eps = 1e-06
SEQ = ("xl", "y", "c")
CHIPS = ("xl", "y")
EXP = ("xh", "z")
bf16 = jnp.bfloat16
f32 = jnp.float32
VMEM_LIMIT = 12 << 20
SWAP = [(0, 1), (1, 0)]
UP = [(i, (i + 1) % 4) for i in range(4)]
DOWN = [(i, (i + 3) % 4) for i in range(4)]
NT = (((1,), (1,)), ((), ()))
NN = (((1,), (0,)), ((), ()))


def mm(a, b, dims=NN):
    return lax.dot_general(a, b, dims, preferred_element_type=f32)


def latent_norm(latent, kv_gain):
    values = latent.astype(f32)
    spread = lax.rsqrt(jnp.mean(values * values, axis=-1, keepdims=True) + eps)
    return (values * spread * kv_gain).astype(bf16)


def start_all(pairs, sems):
    copies = [pltpu.make_async_copy(a, b, sem) for (a, b), sem in zip(pairs, sems)]
    for copy in copies:
        copy.start()
    return copies


def wait_all(copies):
    for copy in copies:
        copy.wait()


STEPS = [(dx, dy) for dx in range(2) for dy in range(4)]


def chip_at(dx, dy):
    return (lax.axis_index("xl") ^ dx) * 4 + ((lax.axis_index("y") + dy) & 3)


def prep_kernel(down_ref, latent_ref, gain_ref, rope_ref, cache_ref, cache_rope_ref, *refs):
    out_refs, (latent, gain, rope, cache, cache_rope, sems) = refs[:-6], refs[-6:]
    units = down_ref.shape[0]
    width = out_refs[0].shape[1]
    small = start_all(
        [
            (latent_ref, latent),
            (gain_ref, gain),
            (rope_ref, rope),
            (cache_ref, cache),
            (cache_rope_ref, cache_rope),
        ],
        [sems.at[i] for i in range(5)],
    )
    large = start_all(
        [
            (
                down_ref.at[:, pl.ds(pl.multiple_of(chip_at(*step) * width, 128), width)],
                ref.at[pl.ds(0, units)],
            )
            for step, ref in zip(STEPS, out_refs)
        ],
        [sems.at[5 + i] for i in range(len(out_refs))],
    )
    wait_all(small)
    slab = latent_norm(latent[...], gain[...])
    count, key_width = cache.shape[0], cache.shape[1] + rope.shape[1]
    blank = jnp.zeros((count, width - key_width), bf16)
    top = jnp.concatenate([cache[...], cache_rope[...], blank], axis=1)
    low = jnp.concatenate([slab, rope[...], blank], axis=1)
    keys = jnp.where(lax.axis_index("z") % 2 == 0, top, low)
    for ref in out_refs:
        ref[units:] = keys
    wait_all(large)


def join_kernel(*refs):
    *piece_refs, down_ref, keys_ref = refs
    units = down_ref.shape[1]
    count = piece_refs[0].shape[0] - units
    for (dx, dy), ref in zip(STEPS, piece_refs):
        j = chip_at(dx, -dy)
        down_ref[j] = ref[:units]
        keys_ref[pl.ds(pl.multiple_of(j * count, count), count), :] = ref[units:]


def route_kernel(
    ids_hbm, gates_hbm, rows_hbm, out_ref, mix_ref, ids, gates, held, sems, *, experts, slots
):
    chip, core = chip_at(0, 0), lax.axis_index("c")
    total, width = out_ref.shape
    padded = total // experts
    top, block = ids.shape
    copies = start_all(
        [
            (ids_hbm, ids),
            (gates_hbm, gates),
            (rows_hbm.at[:, pl.ds(pl.multiple_of(chip * width, 128), width)], held),
        ],
        [sems.at[i] for i in range(3)],
    )
    wait_all(copies[:2])
    names = lax.broadcasted_iota(jnp.int32, (experts, block), 0)
    member = jnp.zeros((experts, block), f32)
    gate = jnp.zeros((experts, block), f32)
    for k in range(top):
        hit = ids[k : k + 1, :] == names
        member = jnp.where(hit, 1.0, member)
        gate = jnp.where(hit, gates[k : k + 1, :], gate)
    before = lax.broadcasted_iota(jnp.int32, (block, block), 0) < lax.broadcasted_iota(
        jnp.int32, (block, block), 1
    )
    rank = mm(member.astype(bf16), jnp.where(before, 1.0, 0.0).astype(bf16))
    place = (member * (rank + 1.0)).astype(bf16)
    slot = lax.broadcasted_iota(jnp.int32, (total, experts), 0)
    start = lax.broadcasted_iota(jnp.int32, (total, experts), 1) * padded
    spread = jnp.where((slot >= start) & (slot < start + padded), 1.0, 0.0).astype(bf16)
    numbers = lax.broadcasted_iota(jnp.int32, (experts, block), 0).astype(bf16)
    first = (core * slots).astype(f32)
    position = lax.broadcasted_iota(jnp.int32, (total, block), 0).astype(f32)
    inside = position - mm(spread, numbers) * padded + 1.0
    take = (mm(spread, place) == inside + first) & (inside < slots + 0.5)
    rest = gate
    for part in range(3):
        piece = rest.astype(bf16)
        rest = rest - piece.astype(f32)
        mix_ref[part] = jnp.where(take, mm(spread, piece), 0.0).astype(bf16)
    wait_all(copies[2:])
    out_ref[...] = mm(jnp.where(take, 1.0, 0.0).astype(bf16), held[...]).astype(bf16)


def slot_rows(slots, padded, count, transposed=False):
    shape = (count // slots * padded, count) if transposed else (count, count // slots * padded)
    small = lax.broadcasted_iota(jnp.int32, shape, 1 if transposed else 0)
    large = lax.broadcasted_iota(jnp.int32, shape, 0 if transposed else 1)
    return jnp.where(small + small // slots * (padded - slots) == large, 1.0, 0.0).astype(bf16)


def compact_kernel(rows_ref, *refs, slots, padded):
    out_ref = refs[-1]
    out_ref[...] = mm(slot_rows(slots, padded, out_ref.shape[0]), rows_ref[...]).astype(bf16)


def stack_kernel(gate_own, gate_other, up_own, up_other, out_ref, sems):
    units = gate_own.shape[0]
    wait_all(
        start_all(
            [
                (ref, out_ref.at[pl.ds(i * units, units)])
                for i, ref in enumerate((gate_own, gate_other, up_own, up_other))
            ],
            [sems.at[i] for i in range(4)],
        )
    )


def add_pieces(piece_refs, places, weight_ref, total):
    for (dx, dy), piece in zip(places, piece_refs):
        width = piece.shape[1]
        column = pl.ds(pl.multiple_of(chip_at(dx, dy) * width, 128), width)
        total += mm(weight_ref[:, column], piece[...], NT)
    return total


def early_kernel(*refs, places):
    *piece_refs, weight_ref, out_ref = refs
    out_ref[...] = add_pieces(piece_refs, places, weight_ref, jnp.zeros(out_ref.shape, f32))


def hidden_kernel(*refs, places):
    *piece_refs, weight_ref, early_ref, out_ref = refs
    total = add_pieces(piece_refs, places, weight_ref, early_ref[...])
    units = total.shape[0] // 2
    gate = total[:units]
    hidden = (gate * jax.nn.sigmoid(gate) * total[units:]).T
    half = hidden.shape[0] // 2
    hidden = jnp.concatenate([hidden[:half], hidden[half:]], axis=1).astype(bf16)
    for j in range(out_ref.shape[0]):
        out_ref[j] = hidden


def down_kernel(hidden_ref, own_ref, other_ref, out_ref, *, slots, padded):
    chips, half, units = hidden_ref.shape
    units = units // 2
    width = out_ref.shape[1]
    low = jnp.zeros((half, width), f32)
    high = jnp.zeros((half, width), f32)
    for j in range(chips):
        weight = jnp.concatenate([own_ref[j], other_ref[j]], axis=0)
        low += mm(hidden_ref[j, :, :units], weight)
        high += mm(hidden_ref[j, :, units:], weight)
    total = jnp.concatenate([low, high], axis=0).astype(bf16)
    out_ref[...] = mm(slot_rows(slots, padded, 2 * half, True), total).astype(bf16)


def combine_kernel(mix_ref, back_ref, keep_ref, send_ref):
    back = back_ref[...]
    dims = (((0,), (0,)), ((), ()))
    total = mm(mix_ref[0], back, dims) + mm(mix_ref[1], back, dims) + mm(mix_ref[2], back, dims)
    half = total.shape[1] // 2
    low, high = total[:, :half], total[:, half:]
    first = lax.axis_index("c") == 0
    keep_ref[...] = jnp.where(first, low, high)
    send_ref[...] = jnp.where(first, high, low).astype(bf16)


def finish_kernel(keep_ref, other_ref, out_ref):
    out_ref[...] = (keep_ref[...] + other_ref[...].astype(f32)).astype(bf16)


def absorb_kernel(nope_hbm, rope_hbm, uk_hbm, out_ref, nope, rope, uk, sems):
    heads, nope_width, latent = uk.shape
    queries = nope.shape[0]
    rope_width = rope.shape[1] // heads
    wait_all(
        start_all(
            [(nope_hbm, nope), (rope_hbm, rope), (uk_hbm, uk)], [sems.at[i] for i in range(3)]
        )
    )
    for h in range(heads):
        rows = slice(h * queries, (h + 1) * queries)
        out_ref[rows, :latent] = mm(
            nope[:, h * nope_width : (h + 1) * nope_width], uk[h]
        ).astype(bf16)
        out_ref[rows, latent:] = rope[:, h * rope_width : (h + 1) * rope_width]


def attend_kernel(query_ref, *refs, first, queries, latent, scale):
    *key_refs, out_ref = refs
    count = key_refs[0].shape[0]
    key_width = query_ref.shape[1]
    rows = out_ref.shape[0]
    core, parity = lax.axis_index("c"), lax.axis_index("z") % 2
    me = chip_at(0, 0) * 2 + core
    key = lax.broadcasted_iota(jnp.int32, (queries, count), 1)
    query = lax.broadcasted_iota(jnp.int32, (queries, count), 0)
    owner, offset = key // queries * 2, key % queries
    bias = []
    for slab in (parity, 1 - parity):
        for part in (core, 1 - core):
            seen = (owner + part < me) | ((owner + part == me) & (offset <= query)) | (slab == 0)
            side = jnp.where(seen, 0.0, -jnp.inf)
            bias.append(jnp.concatenate([side, side], axis=0))
    for g in range(0, rows, 2 * queries):
        full = query_ref[first + g : first + g + 2 * queries]
        scores = [
            mm(full, ref[:, :key_width], NT) * scale + side for ref, side in zip(key_refs, bias)
        ]
        peak = functools.reduce(
            jnp.maximum, [jnp.max(part, axis=1, keepdims=True) for part in scores]
        )
        weights = [jnp.exp(part - peak) for part in scores]
        total = sum(jnp.sum(part, axis=1, keepdims=True) for part in weights)
        mixed = sum(
            mm(part.astype(bf16), ref[:, :latent]) for part, ref in zip(weights, key_refs)
        )
        out_ref[g : g + 2 * queries] = (mixed / total).astype(bf16)


def value_kernel(*refs):
    *mixed_refs, uv_hbm, out_ref, uv, sem = refs
    load = pltpu.make_async_copy(uv_hbm, uv, sem)
    load.start()
    queries = out_ref.shape[0]
    value = uv.shape[2]
    load.wait()
    h = 0
    for ref in mixed_refs:
        for row in range(0, ref.shape[0], queries):
            out_ref[:, h * value : (h + 1) * value] = mm(
                ref[row : row + queries], uv[h]
            ).astype(bf16)
            h += 1


def spec(space=pltpu.VMEM):
    return pl.BlockSpec(memory_space=space)


def pinned(dims, dtype=bf16):
    return pltpu.VMEM(dims, dtype)


def call(kernel, out_shape, *args, scratch=(), flops=0, size=0, name=None):
    spaces = {"v": pltpu.VMEM, "a": pl.ANY, "h": pltpu.HBM}
    arrays = [
        x if space == "a" else pltpu.with_memory_space_constraint(x, spaces[space])
        for x, space in args
    ]
    leaves = lambda x: not isinstance(x, (list, tuple))
    return pl.pallas_call(
        kernel,
        out_shape=out_shape,
        in_specs=[spec(spaces[space]) for _, space in args],
        out_specs=jax.tree.map(lambda _: spec(), out_shape, is_leaf=leaves),
        scratch_shapes=list(scratch),
        compiler_params=pltpu.CompilerParams(vmem_limit_bytes=VMEM_LIMIT),
        cost_estimate=pl.CostEstimate(flops=flops, bytes_accessed=size, transcendentals=0),
        name=name,
    )(*arrays)


def shape(dims, dtype=bf16):
    return jax.ShapeDtypeStruct(dims, dtype)


def exchange(x, axes):
    return lax.all_to_all(x, axes, split_axis=0, concat_axis=0, tiled=True)


def after(x, *others):
    return lax.optimization_barrier((x,) + others)[0]


def per_device(
    q_nope,
    q_rope,
    slab_latent,
    slab_rope,
    kv_gain,
    cache_latent,
    cache_rope,
    w_uk,
    w_uv,
    prev_rows,
    expert_ids,
    gate_scores,
    w_gate,
    w_up,
    w_down,
):
    chips, experts, slots, padded = 8, 16, 12, 16
    units = w_gate.shape[1]
    block, model = prev_rows.shape
    width = model // chips
    count = experts * slots
    cache_len, latent = cache_latent.shape
    rope = cache_rope.shape[1]
    queries = q_nope.shape[0]
    heads, nope, _ = w_uk.shape
    value = w_uv.shape[2]
    top = expert_ids.shape[1]
    DMA = pltpu.SemaphoreType.DMA
    gate_own, up_own, down_own = w_gate[0], w_up[0], w_down[0]

    parts = call(
        prep_kernel,
        [pinned((units + queries, width))] * chips,
        (down_own, "h"),
        (slab_latent, "h"),
        (kv_gain.reshape(1, latent), "h"),
        (slab_rope, "h"),
        (cache_latent, "h"),
        (cache_rope, "h"),
        scratch=[
            pltpu.VMEM((queries, latent), bf16),
            pltpu.VMEM((1, latent), f32),
            pltpu.VMEM((queries, rope), bf16),
            pltpu.VMEM((cache_len, latent), bf16),
            pltpu.VMEM((cache_len, rope), bf16),
            DMA((5 + chips,)),
        ],
        size=4 << 20,
        name="prep",
    )

    def send(part, step):
        pairs = [
            (a * 4 + b, (a ^ step[0]) * 4 + (b + step[1]) % 4) for a in range(2) for b in range(4)
        ]
        return lax.ppermute(part, CHIPS, pairs)

    pieces = [parts[0]] + [send(part, step) for part, step in zip(parts[1:], STEPS[1:])]
    down_mine, keys_mine = call(
        join_kernel,
        [pinned((chips, units, width)), pinned((chips * queries, width))],
        *[(piece, "v") for piece in pieces],
        size=4 << 20,
        name="join",
    )

    outgoing, mix = call(
        functools.partial(route_kernel, experts=experts, slots=slots),
        [pinned((experts * padded, width)), pinned((3, experts * padded, block))],
        (after(expert_ids.T, parts[0]), "h"),
        (gate_scores.T, "h"),
        (prev_rows, "h"),
        scratch=[
            pltpu.VMEM((top, block), jnp.int32),
            pltpu.VMEM((top, block), f32),
            pltpu.VMEM((block, width), bf16),
            DMA((3,)),
        ],
        flops=2 * count * block * width,
        size=1 << 20,
        name="route",
    )
    arrived = exchange(outgoing, EXP)
    query = call(
        absorb_kernel,
        pinned((heads * queries, latent + rope)),
        (q_nope, "h"),
        (q_rope, "h"),
        (w_uk, "h"),
        scratch=[
            pltpu.VMEM(q_nope.shape, bf16),
            pltpu.VMEM(q_rope.shape, bf16),
            pltpu.VMEM(w_uk.shape, bf16),
            DMA((3,)),
        ],
        flops=2 * heads * queries * nope * latent,
        size=2 << 20,
        name="absorb",
    )
    own = call(
        functools.partial(compact_kernel, slots=slots, padded=padded),
        pinned((count, width)),
        (after(arrived, keys_mine, query), "v"),
        size=1 << 19,
        name="compact",
    )

    keys_far = lax.ppermute(keys_mine, "z", [(i, i ^ 1) for i in range(8)])
    down_theirs = lax.ppermute(down_mine, "c", SWAP)
    keys = [
        keys_mine,
        lax.ppermute(keys_mine, "c", SWAP),
        keys_far,
        lax.ppermute(keys_far, "c", SWAP),
    ]
    gate_swap, up_swap = after(gate_own, outgoing), after(up_own, outgoing)
    weights = call(
        stack_kernel,
        pinned((4 * units, model)),
        (gate_own, "h"),
        (lax.ppermute(gate_swap, "c", SWAP), "a"),
        (up_own, "h"),
        (lax.ppermute(up_swap, "c", SWAP), "a"),
        scratch=[DMA((4,))],
        size=8 << 20,
        name="stack",
    )

    across = lax.ppermute(own, "xl", SWAP)
    from_below = lax.ppermute(own, "y", UP)
    from_above = lax.ppermute(own, "y", DOWN)
    across_below = lax.ppermute(across, "y", UP)
    across_above = lax.ppermute(across, "y", DOWN)
    far = lax.ppermute(from_below, "y", UP)
    across_far = lax.ppermute(across_above, "y", DOWN)
    flops = 2 * count * width * 4 * units
    early = call(
        functools.partial(early_kernel, places=[(0, 0), (1, 0), (0, -1), (0, 1)]),
        pinned((4 * units, count), f32),
        *[(piece, "v") for piece in (own, across, from_below, from_above)],
        (weights, "v"),
        flops=4 * flops,
        size=3 << 20,
        name="early",
    )
    hidden = call(
        functools.partial(hidden_kernel, places=[(1, -1), (1, 1), (0, 2), (1, 2)]),
        pinned((chips, count // 2, 4 * units)),
        *[(piece, "v") for piece in (across_below, across_above, far, across_far)],
        (weights, "v"),
        (early, "v"),
        flops=4 * flops,
        size=3 << 20,
        name="hidden",
    )

    def attend(first, last, behind):
        return call(
            functools.partial(
                attend_kernel,
                first=first * queries,
                queries=queries,
                latent=latent,
                scale=(nope + rope) ** (-0.5),
            ),
            pinned(((last - first) * queries, latent)),
            (after(query, behind), "v"),
            *[(part, "v") for part in keys],
            flops=8 * (last - first) * queries * chips * queries * (2 * latent + rope),
            size=4 << 20,
            name="attend",
        )

    mixed_0 = attend(0, 4, hidden)
    produced = call(
        functools.partial(down_kernel, slots=slots, padded=padded),
        pinned((experts * padded, width)),
        (after(exchange(hidden, CHIPS), mixed_0), "v"),
        (down_mine, "v"),
        (down_theirs, "v"),
        flops=2 * count * chips * 2 * units * width,
        size=3 << 20,
        name="down",
    )
    mixed_1 = attend(4, 8, produced)
    attn = call(
        value_kernel,
        shape((queries, heads * value)),
        (mixed_0, "v"),
        (mixed_1, "v"),
        (w_uv, "h"),
        scratch=[pltpu.VMEM(w_uv.shape, bf16), DMA],
        flops=2 * heads * queries * latent * value,
        size=2 << 20,
        name="value",
    )
    keep, send_half = call(
        combine_kernel,
        [pinned((block, width // 2), f32), pinned((block, width // 2))],
        (mix, "v"),
        (after(exchange(produced, EXP), attn), "v"),
        flops=6 * count * block * width,
        size=1 << 19,
        name="combine",
    )
    moe_out = call(
        finish_kernel,
        shape((block, width // 2)),
        (keep, "v"),
        (lax.ppermute(send_half, "c", SWAP), "v"),
        name="finish",
    )
    return attn, moe_out


def solution(mesh):
    fine = Mesh(mesh.devices.reshape(2, 4, 2, 2, 8), SEQ + EXP)
    placed = (
        P(SEQ, EXP),
        P(SEQ, EXP),
        P(SEQ, None),
        P(SEQ, None),
        P(),
        P(SEQ, None),
        P(SEQ, None),
        P(EXP, None, None),
        P(EXP, None, None),
        P(EXP, None),
        P(EXP, None),
        P(EXP, None),
        P(EXP, SEQ, None),
        P(EXP, SEQ, None),
        P(EXP, SEQ, None),
    )
    return jax.shard_map(
        per_device,
        mesh=fine,
        in_specs=placed,
        out_specs=(P(SEQ, EXP), P(EXP, SEQ)),
        check_vma=False,
    )
```

```python
import functools
import jax
import jax.numpy as jnp
from jax import lax
from jax.experimental import pallas as pl
from jax.experimental.pallas import tpu as pltpu
from jax.sharding import Mesh, PartitionSpec as P

eps = 1e-06
SEQ = ("xl", "y", "c")
CHIPS = ("xl", "y")
EXP = ("xh", "z")
bf16 = jnp.bfloat16
f32 = jnp.float32
VMEM_LIMIT = 12 << 20
SWAP = [(0, 1), (1, 0)]
UP = [(i, (i + 1) % 4) for i in range(4)]
DOWN = [(i, (i + 3) % 4) for i in range(4)]
NT = (((1,), (1,)), ((), ()))
NN = (((1,), (0,)), ((), ()))


def mm(a, b, dims=NN):
    return lax.dot_general(a, b, dims, preferred_element_type=f32)


def latent_norm(latent, kv_gain):
    values = latent.astype(f32)
    spread = lax.rsqrt(jnp.mean(values * values, axis=-1, keepdims=True) + eps)
    return (values * spread * kv_gain).astype(bf16)


def start_all(pairs, sems):
    copies = [pltpu.make_async_copy(a, b, sem) for (a, b), sem in zip(pairs, sems)]
    for copy in copies:
        copy.start()
    return copies


def wait_all(copies):
    for copy in copies:
        copy.wait()


EARLY = [(0, 0), (1, 0), (0, -1), (0, 1)]
LATE = [(1, -1), (1, 1), (0, 2), (1, 2)]


def chip_at(dx, dy):
    return (lax.axis_index("xl") ^ dx) * 4 + ((lax.axis_index("y") + dy) & 3)


def prep_kernel(latent_ref, gain_ref, rope_ref, cache_ref, cache_rope_ref, out_ref, *scratch):
    *held, sems = scratch
    hbm = (latent_ref, gain_ref, rope_ref, cache_ref, cache_rope_ref)
    wait_all(start_all(list(zip(hbm, held)), [sems.at[i] for i in range(5)]))
    latent, gain, rope, cache, cache_rope = held
    slab = latent_norm(latent[...], gain[...])
    count, key_width = cache.shape[0], cache.shape[1] + rope.shape[1]
    blank = jnp.zeros((count, out_ref.shape[1] - key_width), bf16)
    out_ref[:count] = jnp.concatenate([cache[...], cache_rope[...], blank], axis=1)
    out_ref[count:] = jnp.concatenate([slab, rope[...], blank], axis=1)


def join_kernel(*refs, places):
    *piece_refs, keys_ref = refs
    count = piece_refs[0].shape[0] // 2
    for place, ref in zip(places, piece_refs):
        row = pl.multiple_of(chip_at(*place) * count, count)
        keys_ref[pl.ds(row, count), :] = ref[:count]
        keys_ref[pl.ds(row + len(places) * count, count), :] = ref[count:]


def route_kernel(
    ids_hbm, gates_hbm, rows_hbm, out_ref, mix_ref, ids, gates, held, sems, *, experts, slots
):
    chip, core = chip_at(0, 0), lax.axis_index("c")
    total = mix_ref.shape[1]
    width = out_ref.shape[2]
    padded = total // experts
    top, block = ids.shape
    copies = start_all(
        [
            (ids_hbm, ids),
            (gates_hbm, gates),
            (rows_hbm.at[:, pl.ds(pl.multiple_of(chip * width, 128), width)], held),
        ],
        [sems.at[i] for i in range(3)],
    )
    wait_all(copies[:2])
    names = lax.broadcasted_iota(jnp.int32, (experts, block), 0)
    member = jnp.zeros((experts, block), f32)
    gate = jnp.zeros((experts, block), f32)
    for k in range(top):
        hit = ids[k : k + 1, :] == names
        member = jnp.where(hit, 1.0, member)
        gate = jnp.where(hit, gates[k : k + 1, :], gate)
    before = lax.broadcasted_iota(jnp.int32, (block, block), 0) < lax.broadcasted_iota(
        jnp.int32, (block, block), 1
    )
    rank = mm(member.astype(bf16), jnp.where(before, 1.0, 0.0).astype(bf16))
    place = (member * (rank + 1.0)).astype(bf16)
    slot = lax.broadcasted_iota(jnp.int32, (total, experts), 0)
    start = lax.broadcasted_iota(jnp.int32, (total, experts), 1) * padded
    spread = jnp.where((slot >= start) & (slot < start + padded), 1.0, 0.0).astype(bf16)
    numbers = lax.broadcasted_iota(jnp.int32, (experts, block), 0).astype(bf16)
    first = (core * slots).astype(f32)
    position = lax.broadcasted_iota(jnp.int32, (total, block), 0).astype(f32)
    inside = position - mm(spread, numbers) * padded + 1.0
    take = (mm(spread, place) == inside + first) & (inside < slots + 0.5)
    rest = gate
    for part in range(3):
        piece = rest.astype(bf16)
        rest = rest - piece.astype(f32)
        mix_ref[part] = jnp.where(take, mm(spread, piece), 0.0).astype(bf16)
    wait_all(copies[2:])
    rows = mm(jnp.where(take, 1.0, 0.0).astype(bf16), held[...]).astype(bf16)
    for e in range(experts):
        out_ref[e] = rows[e * padded : e * padded + slots]


def compact_kernel(rows_ref, out_ref):
    out_ref[...] = jnp.concatenate(
        [rows_ref[e].astype(f32) for e in range(rows_ref.shape[0])], axis=0
    ).astype(bf16)


def stack_kernel(gate_own, gate_other, up_own, up_other, down_own, down_other, *refs):
    in_ref, down_ref, sems = refs
    units = gate_own.shape[0]
    pairs = [
        (ref, in_ref.at[pl.ds(i * units, units)])
        for i, ref in enumerate((gate_own, gate_other, up_own, up_other))
    ] + [
        (ref, down_ref.at[pl.ds(i * units, units)]) for i, ref in enumerate((down_own, down_other))
    ]
    wait_all(start_all(pairs, [sems.at[i] for i in range(6)]))


def add_pieces(piece_refs, places, weight_ref, total):
    for (dx, dy), piece in zip(places, piece_refs):
        width = piece.shape[1]
        column = pl.ds(pl.multiple_of(chip_at(dx, dy) * width, 128), width)
        total += mm(weight_ref[:, column], piece[...], NT)
    return total


def early_kernel(*refs, places):
    *piece_refs, weight_ref, out_ref = refs
    out_ref[...] = add_pieces(piece_refs, places, weight_ref, jnp.zeros(out_ref.shape, f32))


def expert_kernel(*refs, places):
    *piece_refs, weight_ref, early_ref, down_ref, out_ref = refs
    total = add_pieces(piece_refs, places, weight_ref, early_ref[...])
    units = total.shape[0] // 2
    gate = total[:units]
    hidden = (gate * jax.nn.sigmoid(gate) * total[units:]).T.astype(bf16)
    width = out_ref.shape[2]
    for j in range(out_ref.shape[0]):
        out_ref[j] = mm(hidden, down_ref[:, j * width : (j + 1) * width]).astype(bf16)


def total_kernel(parts_ref, out_ref, *, slots, padded):
    total = parts_ref[0].astype(f32)
    for j in range(1, parts_ref.shape[0]):
        total += parts_ref[j].astype(f32)
    out_ref[...] = jnp.zeros_like(out_ref)
    for e in range(total.shape[0] // slots):
        out_ref[e * padded : e * padded + slots] = total[e * slots : (e + 1) * slots].astype(bf16)


def combine_kernel(mix_ref, back_ref, keep_ref, send_ref):
    back = back_ref[...]
    dims = (((0,), (0,)), ((), ()))
    total = mm(mix_ref[0], back, dims) + mm(mix_ref[1], back, dims) + mm(mix_ref[2], back, dims)
    half = total.shape[1] // 2
    low, high = total[:, :half], total[:, half:]
    first = lax.axis_index("c") == 0
    keep_ref[...] = jnp.where(first, low, high)
    send_ref[...] = jnp.where(first, high, low).astype(bf16)


def finish_kernel(keep_ref, other_ref, out_ref):
    out_ref[...] = (keep_ref[...] + other_ref[...].astype(f32)).astype(bf16)


def absorb_kernel(nope_hbm, rope_hbm, uk_hbm, out_ref, nope, rope, uk, sems):
    heads, nope_width, latent = uk.shape
    queries = nope.shape[0]
    rope_width = rope.shape[1] // heads
    wait_all(
        start_all(
            [(nope_hbm, nope), (rope_hbm, rope), (uk_hbm, uk)], [sems.at[i] for i in range(3)]
        )
    )
    for h in range(heads):
        rows = slice(h * queries, (h + 1) * queries)
        out_ref[rows, :latent] = mm(
            nope[:, h * nope_width : (h + 1) * nope_width], uk[h]
        ).astype(bf16)
        out_ref[rows, latent:] = rope[:, h * rope_width : (h + 1) * rope_width]


def attend_kernel(query_ref, *refs, first, queries, latent, scale):
    *key_refs, out_ref = refs
    count = key_refs[0].shape[0] // 2
    key_width = query_ref.shape[1]
    rows = out_ref.shape[0]
    core = lax.axis_index("c")
    me = chip_at(0, 0) * 2 + core
    key = lax.broadcasted_iota(jnp.int32, (queries, count), 1)
    query = lax.broadcasted_iota(jnp.int32, (queries, count), 0)
    owner, offset = key // queries * 2, key % queries
    bias = []
    for part in (core, 1 - core):
        seen = (owner + part < me) | ((owner + part == me) & (offset <= query))
        side = jnp.where(seen, 0.0, -jnp.inf)
        bias.append(jnp.concatenate([side, side], axis=0))
    for g in range(0, rows, 2 * queries):
        full = query_ref[first + g : first + g + 2 * queries]
        scores = []
        for ref, side in zip(key_refs, bias):
            part = mm(full, ref[:, :key_width], NT) * scale
            scores += [part[:, :count], part[:, count:] + side]
        peak = functools.reduce(
            jnp.maximum, [jnp.max(part, axis=1, keepdims=True) for part in scores]
        )
        weights = [jnp.exp(part - peak) for part in scores]
        total = sum(jnp.sum(part, axis=1, keepdims=True) for part in weights)
        mixed = sum(
            mm(jnp.concatenate(weights[2 * i : 2 * i + 2], axis=1).astype(bf16), ref[:, :latent])
            for i, ref in enumerate(key_refs)
        )
        out_ref[g : g + 2 * queries] = (mixed / total).astype(bf16)


def value_kernel(*refs):
    *mixed_refs, uv_hbm, out_ref, uv, sem = refs
    load = pltpu.make_async_copy(uv_hbm, uv, sem)
    load.start()
    queries = out_ref.shape[0]
    value = uv.shape[2]
    load.wait()
    h = 0
    for ref in mixed_refs:
        for row in range(0, ref.shape[0], queries):
            out_ref[:, h * value : (h + 1) * value] = mm(
                ref[row : row + queries], uv[h]
            ).astype(bf16)
            h += 1


def spec(space=pltpu.VMEM):
    return pl.BlockSpec(memory_space=space)


def pinned(dims, dtype=bf16):
    return pltpu.VMEM(dims, dtype)


def call(kernel, out_shape, *args, scratch=(), flops=0, size=0, name=None):
    spaces = {"v": pltpu.VMEM, "a": pl.ANY, "h": pltpu.HBM}
    arrays = [
        x if space == "a" else pltpu.with_memory_space_constraint(x, spaces[space])
        for x, space in args
    ]
    leaves = lambda x: not isinstance(x, (list, tuple))
    return pl.pallas_call(
        kernel,
        out_shape=out_shape,
        in_specs=[spec(spaces[space]) for _, space in args],
        out_specs=jax.tree.map(lambda _: spec(), out_shape, is_leaf=leaves),
        scratch_shapes=list(scratch),
        compiler_params=pltpu.CompilerParams(vmem_limit_bytes=VMEM_LIMIT),
        cost_estimate=pl.CostEstimate(flops=flops, bytes_accessed=size, transcendentals=0),
        name=name,
    )(*arrays)


def shape(dims, dtype=bf16):
    return jax.ShapeDtypeStruct(dims, dtype)


def gathered(x):
    across = lax.ppermute(x, "xl", SWAP)
    below = lax.ppermute(x, "y", UP)
    above = lax.ppermute(x, "y", DOWN)
    early = [x, across, below, above]
    across_below = lax.ppermute(across, "y", UP)
    across_above = lax.ppermute(across, "y", DOWN)
    far = lax.ppermute(below, "y", UP)
    return early, [across_below, across_above, far, lax.ppermute(across_above, "y", DOWN)]


def exchange(x, axes):
    return lax.all_to_all(x, axes, split_axis=0, concat_axis=0, tiled=True)


def after(x, *others):
    return lax.optimization_barrier((x,) + others)[0]


def per_device(
    q_nope,
    q_rope,
    slab_latent,
    slab_rope,
    kv_gain,
    cache_latent,
    cache_rope,
    w_uk,
    w_uv,
    prev_rows,
    expert_ids,
    gate_scores,
    w_gate,
    w_up,
    w_down,
):
    chips, experts, slots, padded = 8, 16, 12, 16
    units = w_gate.shape[1]
    block, model = prev_rows.shape
    width = model // chips
    count = experts * slots
    cache_len, latent = cache_latent.shape
    rope = cache_rope.shape[1]
    queries = q_nope.shape[0]
    heads, nope, _ = w_uk.shape
    value = w_uv.shape[2]
    top = expert_ids.shape[1]
    DMA = pltpu.SemaphoreType.DMA
    gate_own, up_own, down_own = w_gate[0], w_up[0], w_down[0]

    own_keys = call(
        prep_kernel,
        pinned((2 * queries, width)),
        (slab_latent, "h"),
        (kv_gain.reshape(1, latent), "h"),
        (slab_rope, "h"),
        (cache_latent, "h"),
        (cache_rope, "h"),
        scratch=[
            pltpu.VMEM((queries, latent), bf16),
            pltpu.VMEM((1, latent), f32),
            pltpu.VMEM((queries, rope), bf16),
            pltpu.VMEM((cache_len, latent), bf16),
            pltpu.VMEM((cache_len, rope), bf16),
            DMA((5,)),
        ],
        size=1 << 20,
        name="prep",
    )
    early_keys, late_keys = gathered(own_keys)
    keys_mine = call(
        functools.partial(join_kernel, places=EARLY + LATE),
        pinned((2 * chips * queries, width)),
        *[(piece, "v") for piece in early_keys + late_keys],
        size=4 << 20,
        name="join",
    )
    keys = [keys_mine, lax.ppermute(keys_mine, "c", SWAP)]

    outgoing, mix = call(
        functools.partial(route_kernel, experts=experts, slots=slots),
        [pinned((experts, slots, width)), pinned((3, experts * padded, block))],
        (after(expert_ids.T, own_keys), "h"),
        (gate_scores.T, "h"),
        (prev_rows, "h"),
        scratch=[
            pltpu.VMEM((top, block), jnp.int32),
            pltpu.VMEM((top, block), f32),
            pltpu.VMEM((block, width), bf16),
            DMA((3,)),
        ],
        flops=2 * count * block * width,
        size=1 << 20,
        name="route",
    )
    arrived = exchange(outgoing, EXP)
    query = call(
        absorb_kernel,
        pinned((heads * queries, latent + rope)),
        (q_nope, "h"),
        (q_rope, "h"),
        (w_uk, "h"),
        scratch=[
            pltpu.VMEM(q_nope.shape, bf16),
            pltpu.VMEM(q_rope.shape, bf16),
            pltpu.VMEM(w_uk.shape, bf16),
            DMA((3,)),
        ],
        flops=2 * heads * queries * nope * latent,
        size=2 << 20,
        name="absorb",
    )
    own = call(
        compact_kernel,
        pinned((count, width)),
        (after(arrived, keys_mine, query), "v"),
        size=1 << 19,
        name="compact",
    )

    swaps = [
        lax.ppermute(after(w, outgoing), "c", SWAP) for w in (gate_own, up_own, down_own)
    ]
    weights, down = call(
        stack_kernel,
        [pinned((4 * units, model)), pinned((2 * units, model))],
        (gate_own, "h"),
        (swaps[0], "a"),
        (up_own, "h"),
        (swaps[1], "a"),
        (down_own, "h"),
        (swaps[2], "a"),
        scratch=[DMA((6,))],
        size=12 << 20,
        name="stack",
    )

    early_rows, late_rows = gathered(own)
    flops = 2 * count * width * 4 * units
    early = call(
        functools.partial(early_kernel, places=EARLY),
        pinned((4 * units, count), f32),
        *[(piece, "v") for piece in early_rows],
        (weights, "v"),
        flops=4 * flops,
        size=3 << 20,
        name="early",
    )
    partial = call(
        functools.partial(expert_kernel, places=LATE),
        pinned((chips, count, width)),
        *[(piece, "v") for piece in late_rows],
        (weights, "v"),
        (early, "v"),
        (down, "v"),
        flops=6 * flops,
        size=3 << 20,
        name="expert",
    )

    def attend(first, last, behind):
        return call(
            functools.partial(
                attend_kernel,
                first=first * queries,
                queries=queries,
                latent=latent,
                scale=(nope + rope) ** (-0.5),
            ),
            pinned(((last - first) * queries, latent)),
            (after(query, behind), "v"),
            *[(part, "v") for part in keys],
            flops=8 * (last - first) * queries * chips * queries * (2 * latent + rope),
            size=4 << 20,
            name="attend",
        )

    mixed = [attend(0, 4, partial), attend(4, 8, partial)]
    attn = call(
        value_kernel,
        shape((queries, heads * value)),
        *[(part, "v") for part in mixed],
        (w_uv, "h"),
        scratch=[pltpu.VMEM(w_uv.shape, bf16), DMA],
        flops=2 * heads * queries * latent * value,
        size=2 << 20,
        name="value",
    )
    produced = call(
        functools.partial(total_kernel, slots=slots, padded=padded),
        pinned((experts * padded, width)),
        (after(exchange(partial, CHIPS), attn), "v"),
        size=3 << 20,
        name="total",
    )
    keep, send_half = call(
        combine_kernel,
        [pinned((block, width // 2), f32), pinned((block, width // 2))],
        (mix, "v"),
        (exchange(produced, EXP), "v"),
        flops=6 * count * block * width,
        size=1 << 19,
        name="combine",
    )
    moe_out = call(
        finish_kernel,
        shape((block, width // 2)),
        (keep, "v"),
        (lax.ppermute(send_half, "c", SWAP), "v"),
        name="finish",
    )
    return attn, moe_out


def solution(mesh):
    fine = Mesh(mesh.devices.reshape(2, 4, 2, 2, 8), SEQ + EXP)
    placed = (
        P(SEQ, EXP),
        P(SEQ, EXP),
        P(SEQ, None),
        P(SEQ, None),
        P(),
        P(SEQ, None),
        P(SEQ, None),
        P(EXP, None, None),
        P(EXP, None, None),
        P(EXP, None),
        P(EXP, None),
        P(EXP, None),
        P(EXP, SEQ, None),
        P(EXP, SEQ, None),
        P(EXP, SEQ, None),
    )
    return jax.shard_map(
        per_device,
        mesh=fine,
        in_specs=placed,
        out_specs=(P(SEQ, EXP), P(EXP, SEQ)),
        check_vma=False,
    )
```

```python
import functools
import jax
import jax.numpy as jnp
from jax import lax
from jax.experimental import pallas as pl
from jax.experimental.pallas import tpu as pltpu
from jax.sharding import Mesh, PartitionSpec as P

eps = 1e-06
SEQ = ("xl", "y", "c")
CHIPS = ("xl", "y")
EXP = ("xh", "z")
bf16 = jnp.bfloat16
f32 = jnp.float32
VMEM_LIMIT = 12 << 20
SWAP = [(0, 1), (1, 0)]
UP = [(i, (i + 1) % 4) for i in range(4)]
DOWN = [(i, (i + 3) % 4) for i in range(4)]
NT = (((1,), (1,)), ((), ()))
NN = (((1,), (0,)), ((), ()))


def mm(a, b, dims=NN):
    return lax.dot_general(a, b, dims, preferred_element_type=f32)


def latent_norm(latent, kv_gain):
    values = latent.astype(f32)
    spread = lax.rsqrt(jnp.mean(values * values, axis=-1, keepdims=True) + eps)
    return (values * spread * kv_gain).astype(bf16)


def start_all(pairs, sems):
    copies = [pltpu.make_async_copy(a, b, sem) for (a, b), sem in zip(pairs, sems)]
    for copy in copies:
        copy.start()
    return copies


def wait_all(copies):
    for copy in copies:
        copy.wait()


EARLY = [(0, 0), (1, 0), (0, -1), (0, 1)]
LATE = [(1, -1), (1, 1), (0, 2), (1, 2)]


def chip_at(dx, dy):
    return (lax.axis_index("xl") ^ dx) * 4 + ((lax.axis_index("y") + dy) & 3)


def prep_kernel(latent_ref, gain_ref, rope_ref, cache_ref, cache_rope_ref, out_ref, *scratch):
    *held, sems = scratch
    hbm = (latent_ref, gain_ref, rope_ref, cache_ref, cache_rope_ref)
    wait_all(start_all(list(zip(hbm, held)), [sems.at[i] for i in range(5)]))
    latent, gain, rope, cache, cache_rope = held
    slab = latent_norm(latent[...], gain[...])
    count, key_width = cache.shape[0], cache.shape[1] + rope.shape[1]
    blank = jnp.zeros((count, out_ref.shape[1] - key_width), bf16)
    out_ref[:count] = jnp.concatenate([cache[...], cache_rope[...], blank], axis=1)
    out_ref[count:] = jnp.concatenate([slab, rope[...], blank], axis=1)


def join_kernel(*refs, places):
    *piece_refs, keys_ref = refs
    count = piece_refs[0].shape[0] // 2
    for place, ref in zip(places, piece_refs):
        row = pl.multiple_of(chip_at(*place) * count, count)
        keys_ref[pl.ds(row, count), :] = ref[:count]
        keys_ref[pl.ds(row + len(places) * count, count), :] = ref[count:]


def route_kernel(
    ids_hbm, gates_hbm, rows_hbm, out_ref, mix_ref, ids, gates, held, sems, *, experts, slots
):
    chip, core = chip_at(0, 0), lax.axis_index("c")
    total = mix_ref.shape[1]
    width = out_ref.shape[2]
    padded = total // experts
    top, block = ids.shape
    copies = start_all(
        [
            (ids_hbm, ids),
            (gates_hbm, gates),
            (rows_hbm.at[:, pl.ds(pl.multiple_of(chip * width, 128), width)], held),
        ],
        [sems.at[i] for i in range(3)],
    )
    wait_all(copies[:2])
    names = lax.broadcasted_iota(jnp.int32, (experts, block), 0)
    member = jnp.zeros((experts, block), f32)
    gate = jnp.zeros((experts, block), f32)
    for k in range(top):
        hit = ids[k : k + 1, :] == names
        member = jnp.where(hit, 1.0, member)
        gate = jnp.where(hit, gates[k : k + 1, :], gate)
    before = lax.broadcasted_iota(jnp.int32, (block, block), 0) < lax.broadcasted_iota(
        jnp.int32, (block, block), 1
    )
    rank = mm(member.astype(bf16), jnp.where(before, 1.0, 0.0).astype(bf16))
    place = (member * (rank + 1.0)).astype(bf16)
    slot = lax.broadcasted_iota(jnp.int32, (total, experts), 0)
    start = lax.broadcasted_iota(jnp.int32, (total, experts), 1) * padded
    spread = jnp.where((slot >= start) & (slot < start + padded), 1.0, 0.0).astype(bf16)
    numbers = lax.broadcasted_iota(jnp.int32, (experts, block), 0).astype(bf16)
    first = (core * slots).astype(f32)
    position = lax.broadcasted_iota(jnp.int32, (total, block), 0).astype(f32)
    inside = position - mm(spread, numbers) * padded + 1.0
    take = (mm(spread, place) == inside + first) & (inside < slots + 0.5)
    rest = gate
    for part in range(3):
        piece = rest.astype(bf16)
        rest = rest - piece.astype(f32)
        mix_ref[part] = jnp.where(take, mm(spread, piece), 0.0).astype(bf16)
    wait_all(copies[2:])
    rows = mm(jnp.where(take, 1.0, 0.0).astype(bf16), held[...]).astype(bf16)
    for e in range(experts):
        out_ref[e] = rows[e * padded : e * padded + slots]


def compact_kernel(rows_ref, out_ref):
    out_ref[...] = jnp.concatenate(
        [rows_ref[e].astype(f32) for e in range(rows_ref.shape[0])], axis=0
    ).astype(bf16)


def stack_kernel(gate_own, gate_other, up_own, up_other, down_own, down_other, *refs):
    in_ref, down_ref, sems = refs
    units = gate_own.shape[0]
    pairs = [
        (ref, in_ref.at[pl.ds(i * units, units)])
        for i, ref in enumerate((gate_own, gate_other, up_own, up_other))
    ] + [
        (ref, down_ref.at[pl.ds(i * units, units)]) for i, ref in enumerate((down_own, down_other))
    ]
    wait_all(start_all(pairs, [sems.at[i] for i in range(6)]))


def add_pieces(piece_refs, places, weight_ref, total):
    for (dx, dy), piece in zip(places, piece_refs):
        width = piece.shape[1]
        column = pl.ds(pl.multiple_of(chip_at(dx, dy) * width, 128), width)
        total += mm(weight_ref[:, column], piece[...], NT)
    return total


def early_kernel(*refs, places):
    *piece_refs, weight_ref, out_ref = refs
    out_ref[...] = add_pieces(piece_refs, places, weight_ref, jnp.zeros(out_ref.shape, f32))


def expert_kernel(*refs, places):
    *piece_refs, weight_ref, early_ref, down_ref, out_ref = refs
    total = add_pieces(piece_refs, places, weight_ref, early_ref[...])
    units = total.shape[0] // 2
    gate = total[:units]
    hidden = (gate * jax.nn.sigmoid(gate) * total[units:]).T.astype(bf16)
    width = out_ref.shape[2]
    for j in range(out_ref.shape[0]):
        out_ref[j] = mm(hidden, down_ref[:, j * width : (j + 1) * width]).astype(bf16)


def total_kernel(parts_ref, out_ref, *, slots, padded):
    total = parts_ref[0].astype(f32)
    for j in range(1, parts_ref.shape[0]):
        total += parts_ref[j].astype(f32)
    out_ref[...] = jnp.zeros_like(out_ref)
    for e in range(total.shape[0] // slots):
        out_ref[e * padded : e * padded + slots] = total[e * slots : (e + 1) * slots].astype(bf16)


def combine_kernel(mix_ref, back_ref, keep_ref, send_ref):
    back = back_ref[...]
    dims = (((0,), (0,)), ((), ()))
    total = mm(mix_ref[0], back, dims) + mm(mix_ref[1], back, dims) + mm(mix_ref[2], back, dims)
    half = total.shape[1] // 2
    low, high = total[:, :half], total[:, half:]
    first = lax.axis_index("c") == 0
    keep_ref[...] = jnp.where(first, low, high)
    send_ref[...] = jnp.where(first, high, low).astype(bf16)


def finish_kernel(keep_ref, other_ref, out_ref):
    out_ref[...] = (keep_ref[...] + other_ref[...].astype(f32)).astype(bf16)


def absorb_kernel(nope_hbm, rope_hbm, uk_hbm, out_ref, nope, rope, uk, sems):
    heads, nope_width, latent = uk.shape
    queries = nope.shape[0]
    rope_width = rope.shape[1] // heads
    wait_all(
        start_all(
            [(nope_hbm, nope), (rope_hbm, rope), (uk_hbm, uk)], [sems.at[i] for i in range(3)]
        )
    )
    for h in range(heads):
        rows = slice(h * queries, (h + 1) * queries)
        out_ref[rows, :latent] = mm(
            nope[:, h * nope_width : (h + 1) * nope_width], uk[h]
        ).astype(bf16)
        out_ref[rows, latent:] = rope[:, h * rope_width : (h + 1) * rope_width]


def attend_kernel(query_ref, *refs, first, queries, latent, scale):
    *key_refs, out_ref = refs
    count = key_refs[0].shape[0] // 2
    key_width = query_ref.shape[1]
    rows = out_ref.shape[0]
    core = lax.axis_index("c")
    me = chip_at(0, 0) * 2 + core
    key = lax.broadcasted_iota(jnp.int32, (queries, count), 1)
    query = lax.broadcasted_iota(jnp.int32, (queries, count), 0)
    owner, offset = key // queries * 2, key % queries
    bias = []
    for part in (core, 1 - core):
        seen = (owner + part < me) | ((owner + part == me) & (offset <= query))
        side = jnp.where(seen, 0.0, -jnp.inf)
        bias.append(jnp.concatenate([side, side], axis=0))
    for g in range(0, rows, 2 * queries):
        full = query_ref[first + g : first + g + 2 * queries]
        scores = []
        for ref, side in zip(key_refs, bias):
            part = mm(full, ref[:, :key_width], NT) * scale
            scores += [part[:, :count], part[:, count:] + side]
        peak = functools.reduce(
            jnp.maximum, [jnp.max(part, axis=1, keepdims=True) for part in scores]
        )
        weights = [jnp.exp(part - peak) for part in scores]
        total = sum(jnp.sum(part, axis=1, keepdims=True) for part in weights)
        mixed = sum(
            mm(jnp.concatenate(weights[2 * i : 2 * i + 2], axis=1).astype(bf16), ref[:, :latent])
            for i, ref in enumerate(key_refs)
        )
        out_ref[g : g + 2 * queries] = (mixed / total).astype(bf16)


def value_kernel(*refs):
    *mixed_refs, uv_hbm, out_ref, uv, sem = refs
    load = pltpu.make_async_copy(uv_hbm, uv, sem)
    load.start()
    queries = out_ref.shape[0]
    value = uv.shape[2]
    load.wait()
    h = 0
    for ref in mixed_refs:
        for row in range(0, ref.shape[0], queries):
            out_ref[:, h * value : (h + 1) * value] = mm(
                ref[row : row + queries], uv[h]
            ).astype(bf16)
            h += 1


def spec(space=pltpu.VMEM):
    return pl.BlockSpec(memory_space=space)


def pinned(dims, dtype=bf16):
    return pltpu.VMEM(dims, dtype)


def call(kernel, out_shape, *args, scratch=(), flops=0, size=0, name=None):
    spaces = {"v": pltpu.VMEM, "a": pl.ANY, "h": pltpu.HBM}
    arrays = [
        x if space == "a" else pltpu.with_memory_space_constraint(x, spaces[space])
        for x, space in args
    ]
    leaves = lambda x: not isinstance(x, (list, tuple))
    return pl.pallas_call(
        kernel,
        out_shape=out_shape,
        in_specs=[spec(spaces[space]) for _, space in args],
        out_specs=jax.tree.map(lambda _: spec(), out_shape, is_leaf=leaves),
        scratch_shapes=list(scratch),
        compiler_params=pltpu.CompilerParams(vmem_limit_bytes=VMEM_LIMIT),
        cost_estimate=pl.CostEstimate(flops=flops, bytes_accessed=size, transcendentals=0),
        name=name,
    )(*arrays)


def shape(dims, dtype=bf16):
    return jax.ShapeDtypeStruct(dims, dtype)


def gathered(x, in_turn):
    across = lax.ppermute(x, "xl", SWAP)
    below = lax.ppermute(x, "y", UP)
    above = lax.ppermute(x, "y", DOWN)
    early = [x, across, below, above]
    if in_turn:
        across, below, above = lax.optimization_barrier((across, below, above))
    across_below = lax.ppermute(across, "y", UP)
    across_above = lax.ppermute(across, "y", DOWN)
    far = lax.ppermute(below, "y", UP)
    return early, [across_below, across_above, far, lax.ppermute(across_above, "y", DOWN)]


def exchange(x, axes):
    return lax.all_to_all(x, axes, split_axis=0, concat_axis=0, tiled=True)


def after(x, *others):
    return lax.optimization_barrier((x,) + others)[0]


def per_device(
    q_nope,
    q_rope,
    slab_latent,
    slab_rope,
    kv_gain,
    cache_latent,
    cache_rope,
    w_uk,
    w_uv,
    prev_rows,
    expert_ids,
    gate_scores,
    w_gate,
    w_up,
    w_down,
):
    chips, experts, slots, padded = 8, 16, 12, 16
    units = w_gate.shape[1]
    block, model = prev_rows.shape
    width = model // chips
    count = experts * slots
    cache_len, latent = cache_latent.shape
    rope = cache_rope.shape[1]
    queries = q_nope.shape[0]
    heads, nope, _ = w_uk.shape
    value = w_uv.shape[2]
    top = expert_ids.shape[1]
    DMA = pltpu.SemaphoreType.DMA
    gate_own, up_own, down_own = w_gate[0], w_up[0], w_down[0]

    own_keys = call(
        prep_kernel,
        pinned((2 * queries, width)),
        (slab_latent, "h"),
        (kv_gain.reshape(1, latent), "h"),
        (slab_rope, "h"),
        (cache_latent, "h"),
        (cache_rope, "h"),
        scratch=[
            pltpu.VMEM((queries, latent), bf16),
            pltpu.VMEM((1, latent), f32),
            pltpu.VMEM((queries, rope), bf16),
            pltpu.VMEM((cache_len, latent), bf16),
            pltpu.VMEM((cache_len, rope), bf16),
            DMA((5,)),
        ],
        size=1 << 20,
        name="prep",
    )
    early_keys, late_keys = gathered(own_keys, True)
    keys_mine = call(
        functools.partial(join_kernel, places=EARLY + LATE),
        pinned((2 * chips * queries, width)),
        *[(piece, "v") for piece in early_keys + late_keys],
        size=4 << 20,
        name="join",
    )
    keys = [keys_mine, lax.ppermute(keys_mine, "c", SWAP)]

    outgoing, mix = call(
        functools.partial(route_kernel, experts=experts, slots=slots),
        [pinned((experts, slots, width)), pinned((3, experts * padded, block))],
        (after(expert_ids.T, own_keys), "h"),
        (gate_scores.T, "h"),
        (prev_rows, "h"),
        scratch=[
            pltpu.VMEM((top, block), jnp.int32),
            pltpu.VMEM((top, block), f32),
            pltpu.VMEM((block, width), bf16),
            DMA((3,)),
        ],
        flops=2 * count * block * width,
        size=1 << 20,
        name="route",
    )
    arrived = exchange(outgoing, EXP)
    query = call(
        absorb_kernel,
        pinned((heads * queries, latent + rope)),
        (q_nope, "h"),
        (q_rope, "h"),
        (w_uk, "h"),
        scratch=[
            pltpu.VMEM(q_nope.shape, bf16),
            pltpu.VMEM(q_rope.shape, bf16),
            pltpu.VMEM(w_uk.shape, bf16),
            DMA((3,)),
        ],
        flops=2 * heads * queries * nope * latent,
        size=2 << 20,
        name="absorb",
    )
    own = call(
        compact_kernel,
        pinned((count, width)),
        (after(arrived, keys_mine, query), "v"),
        size=1 << 19,
        name="compact",
    )

    swaps = [
        lax.ppermute(after(w, outgoing), "c", SWAP) for w in (gate_own, up_own, down_own)
    ]
    weights, down = call(
        stack_kernel,
        [pinned((4 * units, model)), pinned((2 * units, model))],
        (gate_own, "h"),
        (swaps[0], "a"),
        (up_own, "h"),
        (swaps[1], "a"),
        (down_own, "h"),
        (swaps[2], "a"),
        scratch=[DMA((6,))],
        size=12 << 20,
        name="stack",
    )

    early_rows, late_rows = gathered(own, False)
    flops = 2 * count * width * 4 * units
    early = call(
        functools.partial(early_kernel, places=EARLY),
        pinned((4 * units, count), f32),
        *[(piece, "v") for piece in early_rows],
        (weights, "v"),
        flops=4 * flops,
        size=3 << 20,
        name="early",
    )
    partial = call(
        functools.partial(expert_kernel, places=LATE),
        pinned((chips, count, width)),
        *[(piece, "v") for piece in late_rows],
        (weights, "v"),
        (early, "v"),
        (down, "v"),
        flops=6 * flops,
        size=3 << 20,
        name="expert",
    )

    def attend(first, last, behind):
        return call(
            functools.partial(
                attend_kernel,
                first=first * queries,
                queries=queries,
                latent=latent,
                scale=(nope + rope) ** (-0.5),
            ),
            pinned(((last - first) * queries, latent)),
            (after(query, behind), "v"),
            *[(part, "v") for part in keys],
            flops=8 * (last - first) * queries * chips * queries * (2 * latent + rope),
            size=4 << 20,
            name="attend",
        )

    mixed = [attend(0, 4, partial), attend(4, 8, partial)]
    attn = call(
        value_kernel,
        shape((queries, heads * value)),
        *[(part, "v") for part in mixed],
        (w_uv, "h"),
        scratch=[pltpu.VMEM(w_uv.shape, bf16), DMA],
        flops=2 * heads * queries * latent * value,
        size=2 << 20,
        name="value",
    )
    produced = call(
        functools.partial(total_kernel, slots=slots, padded=padded),
        pinned((experts * padded, width)),
        (after(exchange(partial, CHIPS), attn), "v"),
        size=3 << 20,
        name="total",
    )
    keep, send_half = call(
        combine_kernel,
        [pinned((block, width // 2), f32), pinned((block, width // 2))],
        (mix, "v"),
        (exchange(produced, EXP), "v"),
        flops=6 * count * block * width,
        size=1 << 19,
        name="combine",
    )
    moe_out = call(
        finish_kernel,
        shape((block, width // 2)),
        (keep, "v"),
        (lax.ppermute(send_half, "c", SWAP), "v"),
        name="finish",
    )
    return attn, moe_out


def solution(mesh):
    fine = Mesh(mesh.devices.reshape(2, 4, 2, 2, 8), SEQ + EXP)
    placed = (
        P(SEQ, EXP),
        P(SEQ, EXP),
        P(SEQ, None),
        P(SEQ, None),
        P(),
        P(SEQ, None),
        P(SEQ, None),
        P(EXP, None, None),
        P(EXP, None, None),
        P(EXP, None),
        P(EXP, None),
        P(EXP, None),
        P(EXP, SEQ, None),
        P(EXP, SEQ, None),
        P(EXP, SEQ, None),
    )
    return jax.shard_map(
        per_device,
        mesh=fine,
        in_specs=placed,
        out_specs=(P(SEQ, EXP), P(EXP, SEQ)),
        check_vma=False,
    )
```

```python
import functools
import jax
import jax.numpy as jnp
from jax import lax
from jax.experimental import pallas as pl
from jax.experimental.pallas import tpu as pltpu
from jax.sharding import Mesh, PartitionSpec as P

eps = 1e-06
SEQ = ("xl", "y", "c")
CHIPS = ("xl", "y")
EXP = ("xh", "z")
bf16 = jnp.bfloat16
f32 = jnp.float32
VMEM_LIMIT = 12 << 20
SWAP = [(0, 1), (1, 0)]
UP = [(i, (i + 1) % 4) for i in range(4)]
DOWN = [(i, (i + 3) % 4) for i in range(4)]
NT = (((1,), (1,)), ((), ()))
NN = (((1,), (0,)), ((), ()))


def mm(a, b, dims=NN):
    return lax.dot_general(a, b, dims, preferred_element_type=f32)


def latent_norm(latent, kv_gain):
    values = latent.astype(f32)
    spread = lax.rsqrt(jnp.mean(values * values, axis=-1, keepdims=True) + eps)
    return (values * spread * kv_gain).astype(bf16)


def start_all(pairs, sems):
    copies = [pltpu.make_async_copy(a, b, sem) for (a, b), sem in zip(pairs, sems)]
    for copy in copies:
        copy.start()
    return copies


def wait_all(copies):
    for copy in copies:
        copy.wait()


EARLY = [(0, 0), (1, 0), (0, -1), (0, 1)]
LATE = [(1, -1), (1, 1), (0, 2), (1, 2)]


def chip_at(dx, dy):
    return (lax.axis_index("xl") ^ dx) * 4 + ((lax.axis_index("y") + dy) & 3)


def prep_kernel(latent_ref, gain_ref, rope_ref, cache_ref, cache_rope_ref, out_ref, *scratch):
    *held, sems = scratch
    hbm = (latent_ref, gain_ref, rope_ref, cache_ref, cache_rope_ref)
    wait_all(start_all(list(zip(hbm, held)), [sems.at[i] for i in range(5)]))
    latent, gain, rope, cache, cache_rope = held
    slab = latent_norm(latent[...], gain[...])
    count, key_width = cache.shape[0], cache.shape[1] + rope.shape[1]
    blank = jnp.zeros((count, out_ref.shape[1] - key_width), bf16)
    out_ref[:count] = jnp.concatenate([cache[...], cache_rope[...], blank], axis=1)
    out_ref[count:] = jnp.concatenate([slab, rope[...], blank], axis=1)


def join_kernel(*refs, places):
    *piece_refs, keys_ref = refs
    count = piece_refs[0].shape[0] // 2
    for place, ref in zip(places, piece_refs):
        row = pl.multiple_of(chip_at(*place) * count, count)
        keys_ref[pl.ds(row, count), :] = ref[:count]
        keys_ref[pl.ds(row + len(places) * count, count), :] = ref[count:]


def route_kernel(
    ids_hbm, gates_hbm, rows_hbm, out_ref, mix_ref, ids, gates, held, sems, *, experts, slots
):
    chip, core = chip_at(0, 0), lax.axis_index("c")
    total = mix_ref.shape[1]
    width = out_ref.shape[2]
    padded = total // experts
    top, block = ids.shape
    copies = start_all(
        [
            (ids_hbm, ids),
            (gates_hbm, gates),
            (rows_hbm.at[:, pl.ds(pl.multiple_of(chip * width, 128), width)], held),
        ],
        [sems.at[i] for i in range(3)],
    )
    wait_all(copies[:2])
    names = lax.broadcasted_iota(jnp.int32, (experts, block), 0)
    member = jnp.zeros((experts, block), f32)
    gate = jnp.zeros((experts, block), f32)
    for k in range(top):
        hit = ids[k : k + 1, :] == names
        member = jnp.where(hit, 1.0, member)
        gate = jnp.where(hit, gates[k : k + 1, :], gate)
    before = lax.broadcasted_iota(jnp.int32, (block, block), 0) < lax.broadcasted_iota(
        jnp.int32, (block, block), 1
    )
    rank = mm(member.astype(bf16), jnp.where(before, 1.0, 0.0).astype(bf16))
    place = (member * (rank + 1.0)).astype(bf16)
    slot = lax.broadcasted_iota(jnp.int32, (total, experts), 0)
    start = lax.broadcasted_iota(jnp.int32, (total, experts), 1) * padded
    spread = jnp.where((slot >= start) & (slot < start + padded), 1.0, 0.0).astype(bf16)
    numbers = lax.broadcasted_iota(jnp.int32, (experts, block), 0).astype(bf16)
    first = (core * slots).astype(f32)
    position = lax.broadcasted_iota(jnp.int32, (total, block), 0).astype(f32)
    inside = position - mm(spread, numbers) * padded + 1.0
    take = (mm(spread, place) == inside + first) & (inside < slots + 0.5)
    rest = gate
    for part in range(3):
        piece = rest.astype(bf16)
        rest = rest - piece.astype(f32)
        mix_ref[part] = jnp.where(take, mm(spread, piece), 0.0).astype(bf16)
    wait_all(copies[2:])
    rows = mm(jnp.where(take, 1.0, 0.0).astype(bf16), held[...]).astype(bf16)
    for e in range(experts):
        out_ref[e] = rows[e * padded : e * padded + slots]


def compact_kernel(rows_ref, out_ref):
    out_ref[...] = jnp.concatenate(
        [rows_ref[e].astype(f32) for e in range(rows_ref.shape[0])], axis=0
    ).astype(bf16)


def stack_kernel(gate_own, gate_other, up_own, up_other, down_own, down_other, *refs):
    in_ref, down_ref, sems = refs
    units = gate_own.shape[0]
    pairs = [
        (ref, in_ref.at[pl.ds(i * units, units)])
        for i, ref in enumerate((gate_own, gate_other, up_own, up_other))
    ] + [
        (ref, down_ref.at[pl.ds(i * units, units)]) for i, ref in enumerate((down_own, down_other))
    ]
    wait_all(start_all(pairs, [sems.at[i] for i in range(6)]))


def add_pieces(piece_refs, places, weight_ref, total):
    for (dx, dy), piece in zip(places, piece_refs):
        width = piece.shape[1]
        column = pl.ds(pl.multiple_of(chip_at(dx, dy) * width, 128), width)
        total += mm(weight_ref[:, column], piece[...], NT)
    return total


def early_kernel(*refs, places):
    *piece_refs, weight_ref, out_ref = refs
    out_ref[...] = add_pieces(piece_refs, places, weight_ref, jnp.zeros(out_ref.shape, f32))


def expert_kernel(*refs, places):
    *piece_refs, weight_ref, early_ref, down_ref, out_ref = refs
    total = add_pieces(piece_refs, places, weight_ref, early_ref[...])
    units = total.shape[0] // 2
    gate = total[:units]
    hidden = (gate * jax.nn.sigmoid(gate) * total[units:]).T.astype(bf16)
    width = out_ref.shape[2]
    for j in range(out_ref.shape[0]):
        out_ref[j] = mm(hidden, down_ref[:, j * width : (j + 1) * width]).astype(bf16)


def total_kernel(parts_ref, out_ref, *, slots, padded):
    total = parts_ref[0].astype(f32)
    for j in range(1, parts_ref.shape[0]):
        total += parts_ref[j].astype(f32)
    out_ref[...] = jnp.zeros_like(out_ref)
    for e in range(total.shape[0] // slots):
        out_ref[e * padded : e * padded + slots] = total[e * slots : (e + 1) * slots].astype(bf16)


def combine_kernel(mix_ref, back_ref, keep_ref, send_ref):
    back = back_ref[...]
    dims = (((0,), (0,)), ((), ()))
    total = mm(mix_ref[0], back, dims) + mm(mix_ref[1], back, dims) + mm(mix_ref[2], back, dims)
    half = total.shape[1] // 2
    low, high = total[:, :half], total[:, half:]
    first = lax.axis_index("c") == 0
    keep_ref[...] = jnp.where(first, low, high)
    send_ref[...] = jnp.where(first, high, low).astype(bf16)


def finish_kernel(keep_ref, other_ref, out_ref):
    out_ref[...] = (keep_ref[...] + other_ref[...].astype(f32)).astype(bf16)


def absorb_kernel(nope_hbm, rope_hbm, uk_hbm, out_ref, nope, rope, uk, sems):
    heads, nope_width, latent = uk.shape
    queries = nope.shape[0]
    rope_width = rope.shape[1] // heads
    wait_all(
        start_all(
            [(nope_hbm, nope), (rope_hbm, rope), (uk_hbm, uk)], [sems.at[i] for i in range(3)]
        )
    )
    for h in range(heads):
        rows = slice(h * queries, (h + 1) * queries)
        out_ref[rows, :latent] = mm(
            nope[:, h * nope_width : (h + 1) * nope_width], uk[h]
        ).astype(bf16)
        out_ref[rows, latent:] = rope[:, h * rope_width : (h + 1) * rope_width]


def attend_kernel(query_ref, *refs, first, queries, latent, scale):
    *key_refs, out_ref = refs
    count = key_refs[0].shape[0] // 2
    key_width = query_ref.shape[1]
    rows = out_ref.shape[0]
    core = lax.axis_index("c")
    me = chip_at(0, 0) * 2 + core
    key = lax.broadcasted_iota(jnp.int32, (queries, count), 1)
    query = lax.broadcasted_iota(jnp.int32, (queries, count), 0)
    owner, offset = key // queries * 2, key % queries
    bias = []
    for part in (core, 1 - core):
        seen = (owner + part < me) | ((owner + part == me) & (offset <= query))
        side = jnp.where(seen, 0.0, -jnp.inf)
        bias.append(jnp.concatenate([side, side], axis=0))
    for g in range(0, rows, 2 * queries):
        full = query_ref[first + g : first + g + 2 * queries]
        scores = []
        for ref, side in zip(key_refs, bias):
            part = mm(full, ref[:, :key_width], NT) * scale
            scores += [part[:, :count], part[:, count:] + side]
        peak = functools.reduce(
            jnp.maximum, [jnp.max(part, axis=1, keepdims=True) for part in scores]
        )
        weights = [jnp.exp(part - peak) for part in scores]
        total = sum(jnp.sum(part, axis=1, keepdims=True) for part in weights)
        mixed = sum(
            mm(jnp.concatenate(weights[2 * i : 2 * i + 2], axis=1).astype(bf16), ref[:, :latent])
            for i, ref in enumerate(key_refs)
        )
        out_ref[g : g + 2 * queries] = (mixed / total).astype(bf16)


def value_kernel(*refs):
    *mixed_refs, uv_hbm, out_ref, uv, sem = refs
    load = pltpu.make_async_copy(uv_hbm, uv, sem)
    load.start()
    queries = out_ref.shape[0]
    value = uv.shape[2]
    load.wait()
    h = 0
    for ref in mixed_refs:
        for row in range(0, ref.shape[0], queries):
            out_ref[:, h * value : (h + 1) * value] = mm(
                ref[row : row + queries], uv[h]
            ).astype(bf16)
            h += 1


def spec(space=pltpu.VMEM):
    return pl.BlockSpec(memory_space=space)


def pinned(dims, dtype=bf16):
    return pltpu.VMEM(dims, dtype)


def call(kernel, out_shape, *args, scratch=(), flops=0, size=0, name=None):
    spaces = {"v": pltpu.VMEM, "a": pl.ANY, "h": pltpu.HBM}
    arrays = [
        x if space == "a" else pltpu.with_memory_space_constraint(x, spaces[space])
        for x, space in args
    ]
    leaves = lambda x: not isinstance(x, (list, tuple))
    return pl.pallas_call(
        kernel,
        out_shape=out_shape,
        in_specs=[spec(spaces[space]) for _, space in args],
        out_specs=jax.tree.map(lambda _: spec(), out_shape, is_leaf=leaves),
        scratch_shapes=list(scratch),
        compiler_params=pltpu.CompilerParams(vmem_limit_bytes=VMEM_LIMIT),
        cost_estimate=pl.CostEstimate(flops=flops, bytes_accessed=size, transcendentals=0),
        name=name,
    )(*arrays)


def shape(dims, dtype=bf16):
    return jax.ShapeDtypeStruct(dims, dtype)


def gathered(x, in_turn):
    across = lax.ppermute(x, "xl", SWAP)
    below = lax.ppermute(x, "y", UP)
    above = lax.ppermute(x, "y", DOWN)
    early = [x, across, below, above]
    if in_turn:
        across, below, above = lax.optimization_barrier((across, below, above))
    across_below = lax.ppermute(across, "y", UP)
    across_above = lax.ppermute(across, "y", DOWN)
    far = lax.ppermute(below, "y", UP)
    return early, [across_below, across_above, far, lax.ppermute(across_above, "y", DOWN)]


def exchange(x, axes):
    return lax.all_to_all(x, axes, split_axis=0, concat_axis=0, tiled=True)


def after(x, *others):
    return lax.optimization_barrier((x,) + others)[0]


def per_device(
    q_nope,
    q_rope,
    slab_latent,
    slab_rope,
    kv_gain,
    cache_latent,
    cache_rope,
    w_uk,
    w_uv,
    prev_rows,
    expert_ids,
    gate_scores,
    w_gate,
    w_up,
    w_down,
):
    chips, experts, slots, padded = 8, 16, 12, 16
    units = w_gate.shape[1]
    block, model = prev_rows.shape
    width = model // chips
    count = experts * slots
    cache_len, latent = cache_latent.shape
    rope = cache_rope.shape[1]
    queries = q_nope.shape[0]
    heads, nope, _ = w_uk.shape
    value = w_uv.shape[2]
    top = expert_ids.shape[1]
    DMA = pltpu.SemaphoreType.DMA
    gate_own, up_own, down_own = w_gate[0], w_up[0], w_down[0]

    own_keys = call(
        prep_kernel,
        pinned((2 * queries, width)),
        (slab_latent, "h"),
        (kv_gain.reshape(1, latent), "h"),
        (slab_rope, "h"),
        (cache_latent, "h"),
        (cache_rope, "h"),
        scratch=[
            pltpu.VMEM((queries, latent), bf16),
            pltpu.VMEM((1, latent), f32),
            pltpu.VMEM((queries, rope), bf16),
            pltpu.VMEM((cache_len, latent), bf16),
            pltpu.VMEM((cache_len, rope), bf16),
            DMA((5,)),
        ],
        size=1 << 20,
        name="prep",
    )
    early_keys, late_keys = gathered(own_keys, True)
    keys_mine = call(
        functools.partial(join_kernel, places=EARLY + LATE),
        pinned((2 * chips * queries, width)),
        *[(piece, "v") for piece in early_keys + late_keys],
        size=4 << 20,
        name="join",
    )
    keys = [keys_mine, lax.ppermute(keys_mine, "c", SWAP)]

    outgoing, mix = call(
        functools.partial(route_kernel, experts=experts, slots=slots),
        [pinned((experts, slots, width)), pinned((3, experts * padded, block))],
        (after(expert_ids.T, own_keys), "h"),
        (gate_scores.T, "h"),
        (prev_rows, "h"),
        scratch=[
            pltpu.VMEM((top, block), jnp.int32),
            pltpu.VMEM((top, block), f32),
            pltpu.VMEM((block, width), bf16),
            DMA((3,)),
        ],
        flops=2 * count * block * width,
        size=1 << 20,
        name="route",
    )
    arrived = exchange(outgoing, EXP)
    own = call(
        compact_kernel,
        pinned((count, width)),
        (after(arrived, keys_mine), "v"),
        size=1 << 19,
        name="compact",
    )

    swaps = [
        lax.ppermute(after(w, outgoing), "c", SWAP) for w in (gate_own, up_own, down_own)
    ]
    weights, down = call(
        stack_kernel,
        [pinned((4 * units, model)), pinned((2 * units, model))],
        (gate_own, "h"),
        (swaps[0], "a"),
        (up_own, "h"),
        (swaps[1], "a"),
        (down_own, "h"),
        (swaps[2], "a"),
        scratch=[DMA((6,))],
        size=12 << 20,
        name="stack",
    )

    early_rows, late_rows = gathered(own, False)
    flops = 2 * count * width * 4 * units
    early = call(
        functools.partial(early_kernel, places=EARLY),
        pinned((4 * units, count), f32),
        *[(piece, "v") for piece in early_rows],
        (weights, "v"),
        flops=4 * flops,
        size=3 << 20,
        name="early",
    )
    partial = call(
        functools.partial(expert_kernel, places=LATE),
        pinned((chips, count, width)),
        *[(piece, "v") for piece in late_rows],
        (weights, "v"),
        (early, "v"),
        (down, "v"),
        flops=6 * flops,
        size=3 << 20,
        name="expert",
    )

    query = call(
        absorb_kernel,
        pinned((heads * queries, latent + rope)),
        (after(q_nope, partial), "h"),
        (q_rope, "h"),
        (w_uk, "h"),
        scratch=[
            pltpu.VMEM(q_nope.shape, bf16),
            pltpu.VMEM(q_rope.shape, bf16),
            pltpu.VMEM(w_uk.shape, bf16),
            DMA((3,)),
        ],
        flops=2 * heads * queries * nope * latent,
        size=2 << 20,
        name="absorb",
    )
    def attend(first, last, behind):
        return call(
            functools.partial(
                attend_kernel,
                first=first * queries,
                queries=queries,
                latent=latent,
                scale=(nope + rope) ** (-0.5),
            ),
            pinned(((last - first) * queries, latent)),
            (after(query, behind), "v"),
            *[(part, "v") for part in keys],
            flops=8 * (last - first) * queries * chips * queries * (2 * latent + rope),
            size=4 << 20,
            name="attend",
        )

    mixed = [attend(0, 4, partial), attend(4, 8, partial)]
    attn = call(
        value_kernel,
        shape((queries, heads * value)),
        *[(part, "v") for part in mixed],
        (w_uv, "h"),
        scratch=[pltpu.VMEM(w_uv.shape, bf16), DMA],
        flops=2 * heads * queries * latent * value,
        size=2 << 20,
        name="value",
    )
    produced = call(
        functools.partial(total_kernel, slots=slots, padded=padded),
        pinned((experts * padded, width)),
        (after(exchange(partial, CHIPS), attn), "v"),
        size=3 << 20,
        name="total",
    )
    keep, send_half = call(
        combine_kernel,
        [pinned((block, width // 2), f32), pinned((block, width // 2))],
        (mix, "v"),
        (exchange(produced, EXP), "v"),
        flops=6 * count * block * width,
        size=1 << 19,
        name="combine",
    )
    moe_out = call(
        finish_kernel,
        shape((block, width // 2)),
        (keep, "v"),
        (lax.ppermute(send_half, "c", SWAP), "v"),
        name="finish",
    )
    return attn, moe_out


def solution(mesh):
    fine = Mesh(mesh.devices.reshape(2, 4, 2, 2, 8), SEQ + EXP)
    placed = (
        P(SEQ, EXP),
        P(SEQ, EXP),
        P(SEQ, None),
        P(SEQ, None),
        P(),
        P(SEQ, None),
        P(SEQ, None),
        P(EXP, None, None),
        P(EXP, None, None),
        P(EXP, None),
        P(EXP, None),
        P(EXP, None),
        P(EXP, SEQ, None),
        P(EXP, SEQ, None),
        P(EXP, SEQ, None),
    )
    return jax.shard_map(
        per_device,
        mesh=fine,
        in_specs=placed,
        out_specs=(P(SEQ, EXP), P(EXP, SEQ)),
        check_vma=False,
    )
```
